32 devices in a mesh: band: 2 (over x), tm: 8 (over z, y), space: 2 (over core).
Axes of the slice: x: 2, y: 2, z: 4, core: 2. Of those that a mesh axis runs over, the one named last changes fastest.
Arguments:
- frames: bfloat16 [512, 256, 1024], P('tm', ('band', 'space')), parts along dimension 1, may hold values from -6 to 6
- signal_power: float32 [257], replicated, may hold values from 0.05 to 20
Outputs:
- flow_u: float32 [512, 256, 1024], P('tm', ('band', 'space')), parts along dimension 1
- flow_v: float32 [512, 256, 1024], P('tm', ('band', 'space')), parts along dimension 1
The draws below stay inside these ranges and needn't reach their ends.
There are 2 independent parts, one for each index of `band`. The reference program is written for one: setup_inputs(seed, part) draws one part's arguments, and reference() takes and returns one part's arrays. A program takes and returns all parts, laid end to end along the dimension named above; an argument that names none is the same for every part. Nothing has to cross between parts.
All inputs are finite; a program needn't handle non-finite values.
Results may differ from the reference program's by a relative error of at most 0.0072.
Values may be sent and summed in bfloat16 or wider, within the bound.
A program may use at most 256 MiB of HBM per device.

```python
import math
import jax
import jax.numpy as jnp
from jax import lax

F = 512
W = 1024
ITERS = 3
ROWS = 128


def shard_levels(key, dims, cuts, low, high):
    def one(dim, blocks):
        heights = jax.random.uniform(jax.random.fold_in(jax.random.fold_in(key, 6), dim), (blocks,), jnp.float32, low / len(cuts), high / len(cuts))
        return jnp.repeat(jnp.exp(heights), dims[dim] // blocks).reshape((-1,) + (1,) * (len(dims) - dim - 1))

    loudness = one(*cuts[0])
    for cut in cuts[1:]:
        loudness = loudness * one(*cut)
    return loudness


def gaussian(own_key, dims, deviation, most, cuts=(), kind=jnp.bfloat16):
    entries = jax.random.normal(own_key, dims, jnp.float32) * deviation
    if len(cuts) > 0:
        entries = shard_levels(own_key, dims, cuts, -0.22, 0.18) * entries
    return jnp.clip(entries, min=-most, max=most).astype(kind)


def setup_inputs(seed: int = 0, part: int = 0) -> dict:
    streams_of = jax.random.split(jax.random.key(seed), 3)
    part_keys = jax.random.split(jax.random.fold_in(streams_of[2], part), 3)
    return {
        "frames": gaussian(part_keys[0], (F, ROWS, W), 1.0, 6.0, ((0, 8), (1, 2))),
        "signal_power": jnp.clip(jnp.exp(jax.random.uniform(streams_of[1], (F // 2 + 1,), jnp.float32, math.log(0.05), math.log(20.0))), 0.05, 20.0),
    }


def make_tables():
    freq = jnp.arange(F, dtype=jnp.int32)
    phase = (freq[:, None] * freq[None, :]) % F
    angle = phase.astype(jnp.float32) * (2.0 * math.pi / F)
    return jnp.cos(angle).astype(jnp.bfloat16), jnp.sin(angle).astype(jnp.bfloat16)


def full_power(signal_power):
    return jnp.concatenate([signal_power, signal_power[1:F // 2][::-1]], axis=0)


def wiener_block(block, cosines, sines, power_full):
    real_part = jnp.dot(cosines, block, preferred_element_type=jnp.float32)
    imag_part = jnp.dot(sines, block, preferred_element_type=jnp.float32)
    energy = real_part * real_part + imag_part * imag_part
    noise = jnp.mean(energy[F // 4:3 * F // 4], axis=0) / F + 1e-6
    weight = power_full[:, None] / (power_full[:, None] + noise[None, :])
    scaled_real = (weight * real_part).astype(jnp.bfloat16)
    scaled_imag = (weight * imag_part).astype(jnp.bfloat16)
    restored = jnp.dot(cosines, scaled_real, preferred_element_type=jnp.float32)
    restored = restored + jnp.dot(sines, scaled_imag, preferred_element_type=jnp.float32)
    return (restored / F).astype(jnp.bfloat16)


def across_columns(field):
    padded = jnp.pad(field, ((0, 0), (0, 0), (1, 1)))
    return padded[:, :, 2:] - padded[:, :, :-2]


def across_rows(field):
    padded = jnp.pad(field, ((0, 0), (1, 1), (0, 0)))
    return padded[:, 2:, :] - padded[:, :-2, :]


def neighbour_mean(field):
    row_pad = jnp.pad(field, ((0, 0), (1, 1), (0, 0)))
    col_pad = jnp.pad(field, ((0, 0), (0, 0), (1, 1)))
    return 0.25 * (row_pad[:, :-2, :] + row_pad[:, 2:, :] + col_pad[:, :, :-2] + col_pad[:, :, 2:])


def reference(frames, signal_power):
    cosines, sines = make_tables()
    power_full = full_power(signal_power)
    by_rows = jnp.transpose(frames, (1, 0, 2))
    filtered = lax.map(lambda row_block: wiener_block(row_block, cosines, sines, power_full), by_rows)
    filtered = jnp.transpose(filtered, (1, 0, 2))
    first = filtered.astype(jnp.float32)
    second = jnp.roll(filtered, -1, axis=0).astype(jnp.float32)
    grad_x = 0.25 * (across_columns(first) + across_columns(second))
    grad_y = 0.25 * (across_rows(first) + across_rows(second))
    grad_t = second - first
    denom = 1.0 + grad_x * grad_x + grad_y * grad_y
    flow_u = jnp.zeros_like(first)
    flow_v = jnp.zeros_like(first)
    for iteration in range(ITERS):
        mean_u = neighbour_mean(flow_u)
        mean_v = neighbour_mean(flow_v)
        common = (grad_x * mean_u + grad_y * mean_v + grad_t) / denom
        flow_u = mean_u - grad_x * common
        flow_v = mean_v - grad_y * common
    return flow_u, flow_v
```

```python
import functools
import math

import jax
import jax.numpy as jnp
import numpy as np
from jax import lax
from jax.experimental import pallas as pl
from jax.experimental.pallas import tpu as pltpu
from jax.sharding import PartitionSpec as P

F = 512
ITERS = 3


def from_behind(block, axis, distance):
    devices = range(lax.axis_size(axis))
    route = [((i - distance) % len(devices), i) for i in devices]
    return lax.ppermute(block, axis, route)


def padded_2(block, sides, width):
    for axis, dim in sides:
        count = lax.axis_size(axis)
        forward = [(i, i + 1) for i in range(count - 1)]
        backward = [(target, source) for source, target in forward]
        low = lax.ppermute(
            lax.slice_in_dim(block, block.shape[dim] - width, None, axis=dim), axis, forward
        )
        high = lax.ppermute(lax.slice_in_dim(block, 0, width, axis=dim), axis, backward)
        block = jnp.concatenate([low, block, high], axis=dim)
    return block


def make_tables():
    freq = jnp.arange(F, dtype=jnp.int32)
    phase = freq[:, None] * freq[None, :] % F
    angle = phase.astype(jnp.float32) * (2.0 * math.pi / F)
    return (jnp.cos(angle).astype(jnp.bfloat16), jnp.sin(angle).astype(jnp.bfloat16))


def full_power(signal_power):
    return jnp.concatenate([signal_power, signal_power[1 : F // 2][::-1]], axis=0)


def wiener_block(block, cosines, sines, power_full):
    real_part = jnp.dot(cosines, block, preferred_element_type=jnp.float32)
    imag_part = jnp.dot(sines, block, preferred_element_type=jnp.float32)
    energy = real_part * real_part + imag_part * imag_part
    noise = jnp.mean(energy[F // 4 : 3 * F // 4], axis=0) / F + 1e-06
    weight = power_full[:, None] / (power_full[:, None] + noise[None, :])
    scaled_real = (weight * real_part).astype(jnp.bfloat16)
    scaled_imag = (weight * imag_part).astype(jnp.bfloat16)
    restored = jnp.dot(cosines, scaled_real, preferred_element_type=jnp.float32)
    restored = restored + jnp.dot(sines, scaled_imag, preferred_element_type=jnp.float32)
    return (restored / F).astype(jnp.bfloat16)


def across_columns(field):
    padded = jnp.pad(field, ((0, 0), (0, 0), (1, 1)))
    return padded[:, :, 2:] - padded[:, :, :-2]


def vertical_mean(extended):
    center = extended[:, 1:-1, :]
    col_pad = jnp.pad(center, ((0, 0), (0, 0), (1, 1)))
    return 0.25 * (
        extended[:, :-2, :] + extended[:, 2:, :] + col_pad[:, :, :-2] + col_pad[:, :, 2:]
    )


def derivatives(extended_pair):
    first = extended_pair[0].astype(jnp.float32)
    second = extended_pair[1].astype(jnp.float32)
    first_mid = first[:, 1:-1, :]
    second_mid = second[:, 1:-1, :]
    grad_x = 0.25 * (across_columns(first_mid) + across_columns(second_mid))
    grad_y = 0.25 * (first[:, 2:, :] - first[:, :-2, :] + (second[:, 2:, :] - second[:, :-2, :]))
    grad_t = second_mid - first_mid
    denom = 1.0 + grad_x * grad_x + grad_y * grad_y
    return (grad_x, grad_y, grad_t, denom)


def plain_shards(frames, signal_power):
    cosines, sines = make_tables()
    power_full = full_power(signal_power)
    gathered = lax.all_to_all(frames, "tm", split_axis=1, concat_axis=0, tiled=True)
    shape_now = gathered.shape
    flat = gathered.reshape(shape_now[0], shape_now[1] * shape_now[2])
    restored = lax.all_to_all(
        wiener_block(flat, cosines, sines, power_full).reshape(shape_now),
        "tm",
        split_axis=0,
        concat_axis=1,
        tiled=True,
    )
    following = from_behind(restored[0], "tm", -1)
    upcoming = jnp.concatenate([restored[1:], following[None]], axis=0)
    frame_pair = jnp.stack([restored, upcoming], axis=0)
    extended_pair = padded_2(frame_pair, (("space", 2),), 1)
    grad_x, grad_y, grad_t, denom = derivatives(extended_pair)
    flow_u = jnp.zeros_like(grad_x)
    flow_v = jnp.zeros_like(grad_x)
    for iteration in range(ITERS):
        if iteration == 0:
            mean_u = vertical_mean(jnp.pad(flow_u, ((0, 0), (1, 1), (0, 0))))
            mean_v = vertical_mean(jnp.pad(flow_v, ((0, 0), (1, 1), (0, 0))))
        else:
            extended_flow = padded_2(jnp.stack([flow_u, flow_v], axis=0), (("space", 2),), 1)
            mean_u = vertical_mean(extended_flow[0])
            mean_v = vertical_mean(extended_flow[1])
        common = (grad_x * mean_u + grad_y * mean_v + grad_t) / denom
        flow_u = mean_u - grad_x * common
        flow_v = mean_v - grad_y * common
    return (flow_u, flow_v)


MESH = pl.DeviceIdType.MESH


def real_basis():
    freq = np.arange(F)
    angle = (freq[:, None] * freq[None, :] % F).astype(np.float32) * np.float32(2.0 * math.pi / F)
    half = F // 2
    basis = np.concatenate(
        [np.cos(angle[:half]), np.cos(angle[half : half + 1]), np.sin(angle[1:half])], axis=0
    ).astype(jnp.bfloat16)
    weight = np.full((F,), 2.0 / F, np.float32)
    weight[0] = weight[half] = 1.0 / F
    inverse = (basis.astype(np.float32) * weight[:, None]).T.astype(jnp.bfloat16)
    return basis, np.ascontiguousarray(inverse)


def filter_tile(block, basis, inverse, power):
    half, quarter = F // 2, F // 4
    spectrum = jnp.dot(basis, block, preferred_element_type=jnp.float32)
    energy = spectrum * spectrum
    upper = energy[quarter:half] + energy[half + quarter :]
    total = 2.0 * jnp.sum(upper, axis=0, keepdims=True) - upper[0:1] + energy[half : half + 1]
    noise = total * (1.0 / (half * F)) + 1e-06
    scaled = (power / (power + noise) * spectrum).astype(jnp.bfloat16)
    return jnp.dot(inverse, scaled, preferred_element_type=jnp.float32).astype(jnp.bfloat16)


def exchange_kernel(n, x_ref, basis_ref, inverse_ref, power_ref, out_ref, gath, filt, s1, r1, s2, r2):
    me = lax.axis_index("tm")
    rows, frames, columns = x_ref.shape
    chunks = rows // n
    tile = power_ref.shape[1]

    barrier = pltpu.get_barrier_semaphore()
    for d in range(1, n):
        peer = lax.rem(me + d, n)
        pl.semaphore_signal(barrier, inc=1, device_id={"tm": peer}, device_id_type=MESH)
    pl.semaphore_wait(barrier, n - 1)

    def span(device):
        return pl.ds(pl.multiple_of(device * frames, frames), frames)

    def scatter(c, carry):
        pltpu.make_async_copy(x_ref.at[c * n + me], gath.at[c, span(me)], r1.at[c]).start()
        for d in range(1, n):
            peer = lax.rem(me + d, n)
            pltpu.make_async_remote_copy(
                src_ref=x_ref.at[c * n + peer],
                dst_ref=gath.at[c, span(me)],
                send_sem=s1.at[c],
                recv_sem=r1.at[c],
                device_id={"tm": peer},
                device_id_type=MESH,
            ).start()
        return carry

    lax.fori_loop(0, chunks, scatter, 0)

    def work(c, carry):
        pltpu.make_async_copy(gath.at[c], gath.at[c], r1.at[c]).wait()

        def one(i, carry):
            cols = pl.ds(pl.multiple_of(i * tile, tile), tile)
            filt[c, :, cols] = filter_tile(
                gath[c, :, cols], basis_ref[...], inverse_ref[...], power_ref[...]
            )
            return carry

        lax.fori_loop(0, columns // tile, one, 0)
        pltpu.make_async_copy(filt.at[c, span(me)], out_ref.at[c * n + me], r2.at[c]).start()
        for d in range(1, n):
            peer = lax.rem(me + d, n)
            pltpu.make_async_remote_copy(
                src_ref=filt.at[c, span(peer)],
                dst_ref=out_ref.at[c * n + me],
                send_sem=s2.at[c],
                recv_sem=r2.at[c],
                device_id={"tm": peer},
                device_id_type=MESH,
            ).start()
        return carry

    lax.fori_loop(0, chunks, work, 0)

    def drain(c, carry):
        sent = gath.at[c, pl.ds(0, (n - 1) * frames)]
        pltpu.make_async_copy(sent, sent, s1.at[c]).wait()
        pltpu.make_async_copy(sent, sent, s2.at[c]).wait()
        landed = out_ref.at[pl.ds(c * n, n)]
        pltpu.make_async_copy(landed, landed, r2.at[c]).wait()
        return carry

    lax.fori_loop(0, chunks, drain, 0)


def exchange_and_filter(by_rows, signal_power):
    n = lax.axis_size("tm")
    rows, frames, columns = by_rows.shape
    chunks, half, tile = rows // n, F // 2, 256
    basis, inverse = real_basis()
    power = jnp.concatenate([signal_power, signal_power[1:half]], axis=0)
    power = jnp.broadcast_to(power[:, None], (F, tile))
    vmem = pl.BlockSpec(memory_space=pltpu.VMEM)
    hbm = pl.BlockSpec(memory_space=pl.ANY)
    return pl.pallas_call(
        functools.partial(exchange_kernel, n),
        out_shape=jax.ShapeDtypeStruct(by_rows.shape, jnp.bfloat16),
        in_specs=[hbm, vmem, vmem, vmem],
        out_specs=hbm,
        scratch_shapes=[
            pltpu.VMEM((chunks, F, columns), jnp.bfloat16),
            pltpu.VMEM((chunks, F, columns), jnp.bfloat16),
        ]
        + [pltpu.SemaphoreType.DMA((chunks,))] * 4,
        compiler_params=pltpu.CompilerParams(
            collective_id=0, has_side_effects=True, vmem_limit_bytes=40 * 2**20
        ),
        cost_estimate=pl.CostEstimate(
            flops=4 * F * rows * frames * columns,
            bytes_accessed=4 * rows * frames * columns,
            transcendentals=0,
        ),
        name="exchange",
    )(by_rows, jnp.asarray(basis), jnp.asarray(inverse), power)


STRIP = 16
LAG = 8


def flow_kernel(flag_ref, body_ref, low_ref, high_ref, next_ref, u_ref, v_ref, *ring):
    total, shift, gx_r, gy_r, gt_r, inv_r, u1_r, v1_r, u2_r, v2_r, u3_r, v3_r = ring
    rows, strip, columns = body_ref.shape
    groups = rows // LAG + 1
    lane = lax.broadcasted_iota(jnp.int32, (strip, columns), 1)
    frame = lax.broadcasted_iota(jnp.int32, (strip, columns), 0)
    at_low, at_high, at_last = lane == 0, lane == columns - 1, frame == strip - 1
    low_flag, high_flag = flag_ref[0], flag_ref[1]

    def left(x):
        return jnp.where(at_low, 0.0, pltpu.roll(x, 1, 1))

    def right(x):
        return jnp.where(at_high, 0.0, pltpu.roll(x, columns - 1, 1))

    def mean(ref, i):
        center = ref[i % LAG]
        return 0.25 * (ref[(i - 1) % LAG] + ref[(i + 1) % LAG] + left(center) + right(center))

    def step(u_prev, v_prev, i):
        mean_u, mean_v = mean(u_prev, i), mean(v_prev, i)
        j = i % LAG
        gx, gy = gx_r[j], gy_r[j]
        common = (gx * mean_u + gy * mean_v + gt_r[j]) * inv_r[j]
        return mean_u - gx * common, mean_v - gy * common

    def group(g, carry):
        for i in range(LAG):
            at = jnp.clip(g * LAG + i - 5, 0, rows - 1)
            first = body_ref[at]
            if 2 <= i <= 4:
                first = jnp.where(g == 0, low_ref[i - 2], first)
            if i >= 5:
                first = jnp.where(g == groups - 1, high_ref[i - 5], first)
            first = first.astype(jnp.float32)
            extended = jnp.clip(g * LAG + i - 2, 0, rows + 5)
            after = next_ref[0, pl.ds(extended, 1), :]
            second = jnp.where(at_last, after, pltpu.roll(first, strip - 1, 0))
            total[(i - 2) % LAG] = first + second
            shift[(i - 2) % LAG] = second - first
            k = (i - 3) % LAG
            center = total[k]
            gx = 0.25 * (right(center) - left(center))
            gy = 0.25 * (total[(i - 2) % LAG] - total[(i - 4) % LAG])
            gt = shift[k]
            inv = 1.0 / (1.0 + gx * gx + gy * gy)
            common = gt * inv
            gx_r[k], gy_r[k], gt_r[k], inv_r[k] = gx, gy, gt, inv
            u1_r[k] = -gx * common
            v1_r[k] = -gy * common
            k = (i - 4) % LAG
            u2, v2 = step(u1_r, v1_r, i - 4)
            if i == 6:
                keep = jnp.where(g == 0, low_flag, 1.0)
                u2, v2 = u2 * keep, v2 * keep
            if i == 7:
                keep = jnp.where(g == groups - 1, high_flag, 1.0)
                u2, v2 = u2 * keep, v2 * keep
            u2_r[k], v2_r[k] = u2, v2
            u3_r[i], v3_r[i] = step(u2_r, v2_r, i - 5)

        @pl.when(g > 0)
        def _():
            place = pl.ds(pl.multiple_of((g - 1) * LAG, LAG), LAG)
            for b in range(0, strip, 8):
                u_ref[b : b + 8, place, :] = jnp.swapaxes(u3_r[:, b : b + 8, :], 0, 1)
                v_ref[b : b + 8, place, :] = jnp.swapaxes(v3_r[:, b : b + 8, :], 0, 1)

        return carry

    lax.fori_loop(0, groups, group, 0)


def flow(body, low, high, following, flags):
    rows, frames, columns = body.shape
    out = jax.ShapeDtypeStruct((frames, rows, columns), jnp.float32)
    out_spec = pl.BlockSpec((STRIP, rows, columns), lambda i: (i, 0, 0))

    def strip_of(height):
        return pl.BlockSpec((height, STRIP, columns), lambda i: (0, i, 0))

    return pl.pallas_call(
        flow_kernel,
        grid=(frames // STRIP,),
        out_shape=(out, out),
        in_specs=[
            pl.BlockSpec(memory_space=pltpu.SMEM),
            strip_of(rows),
            strip_of(3),
            strip_of(3),
            pl.BlockSpec((1, following.shape[1], columns), lambda i: (i, 0, 0)),
        ],
        out_specs=(out_spec, out_spec),
        scratch_shapes=[pltpu.VMEM((LAG, STRIP, columns), jnp.float32)] * 12,
        compiler_params=pltpu.CompilerParams(vmem_limit_bytes=56 * 2**20),
        cost_estimate=pl.CostEstimate(
            flops=100 * rows * frames * columns,
            bytes_accessed=10 * rows * frames * columns,
            transcendentals=0,
        ),
        name="flow",
    )(flags, body, low, high, following)


def neighbours(block, dim, width):
    count = lax.axis_size("space")
    forward = [(i, i + 1) for i in range(count - 1)]
    backward = [(target, source) for source, target in forward]
    size = block.shape[dim]
    low = lax.ppermute(
        lax.slice_in_dim(block, size - width, size, axis=dim), "space", forward
    )
    high = lax.ppermute(lax.slice_in_dim(block, 0, width, axis=dim), "space", backward)
    return low, high


def shards(frames, signal_power):
    n = lax.axis_size("tm")
    count, rows, columns = frames.shape
    fits = n > 1 and count % STRIP == 0 and rows % n == 0 and rows % LAG == 0
    if not (fits and columns % 256 == 0):
        return plain_shards(frames, signal_power)
    by_rows = jnp.transpose(frames, (1, 0, 2))
    body = exchange_and_filter(by_rows, signal_power)
    following = from_behind(body[:, 0], "tm", -1)
    firsts = [body[:, b] for b in range(STRIP, count, STRIP)] + [following]
    firsts = jnp.stack(firsts, axis=0)
    low, high = neighbours(body, 0, 3)
    low_first, high_first = neighbours(firsts, 1, 3)
    firsts = jnp.concatenate([low_first, firsts, high_first], axis=1).astype(jnp.float32)
    here, last = lax.axis_index("space"), lax.axis_size("space") - 1
    flags = jnp.stack([here > 0, here < last]).astype(jnp.float32)
    return flow(body, low, high, firsts, flags)


def solution(mesh):
    in_specs = (P("tm", ("band", "space"), None), P())
    out_specs = (P("tm", ("band", "space"), None), P("tm", ("band", "space"), None))
    return jax.shard_map(shards, mesh=mesh, in_specs=in_specs, out_specs=out_specs, check_vma=False)
```

```python
import functools
import math

import jax
import jax.numpy as jnp
import numpy as np
from jax import lax
from jax.experimental import pallas as pl
from jax.experimental.pallas import tpu as pltpu
from jax.sharding import PartitionSpec as P

F = 512
ITERS = 3


def from_behind(block, axis, distance):
    devices = range(lax.axis_size(axis))
    route = [((i - distance) % len(devices), i) for i in devices]
    return lax.ppermute(block, axis, route)


def padded_2(block, sides, width):
    for axis, dim in sides:
        count = lax.axis_size(axis)
        forward = [(i, i + 1) for i in range(count - 1)]
        backward = [(target, source) for source, target in forward]
        low = lax.ppermute(
            lax.slice_in_dim(block, block.shape[dim] - width, None, axis=dim), axis, forward
        )
        high = lax.ppermute(lax.slice_in_dim(block, 0, width, axis=dim), axis, backward)
        block = jnp.concatenate([low, block, high], axis=dim)
    return block


def make_tables():
    freq = jnp.arange(F, dtype=jnp.int32)
    phase = freq[:, None] * freq[None, :] % F
    angle = phase.astype(jnp.float32) * (2.0 * math.pi / F)
    return (jnp.cos(angle).astype(jnp.bfloat16), jnp.sin(angle).astype(jnp.bfloat16))


def full_power(signal_power):
    return jnp.concatenate([signal_power, signal_power[1 : F // 2][::-1]], axis=0)


def wiener_block(block, cosines, sines, power_full):
    real_part = jnp.dot(cosines, block, preferred_element_type=jnp.float32)
    imag_part = jnp.dot(sines, block, preferred_element_type=jnp.float32)
    energy = real_part * real_part + imag_part * imag_part
    noise = jnp.mean(energy[F // 4 : 3 * F // 4], axis=0) / F + 1e-06
    weight = power_full[:, None] / (power_full[:, None] + noise[None, :])
    scaled_real = (weight * real_part).astype(jnp.bfloat16)
    scaled_imag = (weight * imag_part).astype(jnp.bfloat16)
    restored = jnp.dot(cosines, scaled_real, preferred_element_type=jnp.float32)
    restored = restored + jnp.dot(sines, scaled_imag, preferred_element_type=jnp.float32)
    return (restored / F).astype(jnp.bfloat16)


def across_columns(field):
    padded = jnp.pad(field, ((0, 0), (0, 0), (1, 1)))
    return padded[:, :, 2:] - padded[:, :, :-2]


def vertical_mean(extended):
    center = extended[:, 1:-1, :]
    col_pad = jnp.pad(center, ((0, 0), (0, 0), (1, 1)))
    return 0.25 * (
        extended[:, :-2, :] + extended[:, 2:, :] + col_pad[:, :, :-2] + col_pad[:, :, 2:]
    )


def derivatives(extended_pair):
    first = extended_pair[0].astype(jnp.float32)
    second = extended_pair[1].astype(jnp.float32)
    first_mid = first[:, 1:-1, :]
    second_mid = second[:, 1:-1, :]
    grad_x = 0.25 * (across_columns(first_mid) + across_columns(second_mid))
    grad_y = 0.25 * (first[:, 2:, :] - first[:, :-2, :] + (second[:, 2:, :] - second[:, :-2, :]))
    grad_t = second_mid - first_mid
    denom = 1.0 + grad_x * grad_x + grad_y * grad_y
    return (grad_x, grad_y, grad_t, denom)


def plain_shards(frames, signal_power):
    cosines, sines = make_tables()
    power_full = full_power(signal_power)
    gathered = lax.all_to_all(frames, "tm", split_axis=1, concat_axis=0, tiled=True)
    shape_now = gathered.shape
    flat = gathered.reshape(shape_now[0], shape_now[1] * shape_now[2])
    restored = lax.all_to_all(
        wiener_block(flat, cosines, sines, power_full).reshape(shape_now),
        "tm",
        split_axis=0,
        concat_axis=1,
        tiled=True,
    )
    following = from_behind(restored[0], "tm", -1)
    upcoming = jnp.concatenate([restored[1:], following[None]], axis=0)
    frame_pair = jnp.stack([restored, upcoming], axis=0)
    extended_pair = padded_2(frame_pair, (("space", 2),), 1)
    grad_x, grad_y, grad_t, denom = derivatives(extended_pair)
    flow_u = jnp.zeros_like(grad_x)
    flow_v = jnp.zeros_like(grad_x)
    for iteration in range(ITERS):
        if iteration == 0:
            mean_u = vertical_mean(jnp.pad(flow_u, ((0, 0), (1, 1), (0, 0))))
            mean_v = vertical_mean(jnp.pad(flow_v, ((0, 0), (1, 1), (0, 0))))
        else:
            extended_flow = padded_2(jnp.stack([flow_u, flow_v], axis=0), (("space", 2),), 1)
            mean_u = vertical_mean(extended_flow[0])
            mean_v = vertical_mean(extended_flow[1])
        common = (grad_x * mean_u + grad_y * mean_v + grad_t) / denom
        flow_u = mean_u - grad_x * common
        flow_v = mean_v - grad_y * common
    return (flow_u, flow_v)


MESH = pl.DeviceIdType.MESH


def real_basis():
    freq = np.arange(F)
    angle = (freq[:, None] * freq[None, :] % F).astype(np.float32) * np.float32(2.0 * math.pi / F)
    half = F // 2
    basis = np.concatenate(
        [np.cos(angle[:half]), np.cos(angle[half : half + 1]), np.sin(angle[1:half])], axis=0
    ).astype(jnp.bfloat16)
    weight = np.full((F,), 2.0 / F, np.float32)
    weight[0] = weight[half] = 1.0 / F
    inverse = (basis.astype(np.float32) * weight[:, None]).T.astype(jnp.bfloat16)
    return basis, np.ascontiguousarray(inverse)


STRIP = 16
RING = 4
TILE = 256


def filter_tile(block, basis, inverse, power):
    half, quarter = F // 2, F // 4
    spectrum = jnp.dot(basis, block, preferred_element_type=jnp.float32)
    energy = spectrum * spectrum
    upper = energy[quarter:half] + energy[half + quarter :]
    total = 2.0 * jnp.sum(upper, axis=0, keepdims=True) - upper[0:1] + energy[half : half + 1]
    noise = total * (1.0 / (half * F)) + 1e-06
    scaled = (power / (power + noise) * spectrum).astype(jnp.bfloat16)
    return jnp.dot(inverse, scaled, preferred_element_type=jnp.float32)


def fused_kernel(n, x_ref, basis_ref, inverse_ref, power_ref, u_ref, v_ref, *scratch):
    (xin, xt, gath, filt, land, edge, after, land_h, after_h) = scratch[:9]
    (total, shift, gx_r, gy_r, gt_r, inv_r, u1_r, v1_r, u2_r, v2_r) = scratch[9:19]
    (sx, s1, r1, s2, r2, s3, r3, sh, rh, so) = scratch[19:]
    me, side = lax.axis_index("tm"), lax.axis_index("space")
    frames, rows, columns = x_ref.shape
    chunks, blocks, strips = rows // n, rows // STRIP, frames // STRIP
    per_block = chunks // blocks

    def physical(row):
        return side * row + (1 - side) * (rows - 1 - row)

    def block_rows(m):
        first = side * m + (1 - side) * (blocks - 1 - m)
        return pl.ds(pl.multiple_of(first * STRIP, STRIP), STRIP)

    def span(device):
        return pl.ds(pl.multiple_of(device * frames, frames), frames)

    def fetch(m):
        slot = lax.rem(m, 2)
        return pltpu.make_async_copy(x_ref.at[:, block_rows(m), :], xin.at[slot], sx.at[slot])

    fetch(0).start()
    fetch(1).start()
    barrier = pltpu.get_barrier_semaphore()
    for d in range(1, n):
        peer = lax.rem(me + d, n)
        pl.semaphore_signal(barrier, inc=1, device_id={"tm": peer}, device_id_type=MESH)
    pl.semaphore_signal(barrier, inc=1, device_id={"space": 1 - side}, device_id_type=MESH)
    pl.semaphore_wait(barrier, n)

    def to_peer(src, dst, send, recv, peer):
        return pltpu.make_async_remote_copy(
            src_ref=src,
            dst_ref=dst,
            send_sem=send,
            recv_sem=recv,
            device_id={"tm": peer},
            device_id_type=MESH,
        )

    def scatter(m, carry):
        fetch(m).wait()
        slot = lax.rem(m, 2)
        per_row = columns // TILE

        def turn(i, carry):
            cols = pl.ds(pl.multiple_of(lax.rem(i, per_row) * TILE, TILE), TILE)
            part = pl.ds(pl.multiple_of(i // per_row * STRIP, STRIP), STRIP)
            piece = xin[slot, part, :, cols].astype(jnp.float32)
            xt[block_rows(m), part, cols] = jnp.swapaxes(piece, 0, 1).astype(jnp.bfloat16)
            return carry

        lax.fori_loop(0, strips * per_row, turn, 0)

        @pl.when(m + 2 < blocks)
        def _():
            fetch(m + 2).start()

        for k in range(per_block):
            c = m * per_block + k
            own = xt.at[physical(c * n + me)]
            pltpu.make_async_copy(own, gath.at[c, span(me)], r1.at[c]).start()
            for d in range(1, n):
                peer = lax.rem(me + d, n)
                src = xt.at[physical(c * n + peer)]
                to_peer(src, gath.at[c, span(me)], s1.at[c], r1.at[c], peer).start()
        return carry

    lax.fori_loop(0, blocks, scatter, 0)

    def work(c, carry):
        pltpu.make_async_copy(gath.at[c], gath.at[c], r1.at[c]).wait()

        def one(i, carry):
            cols = pl.ds(pl.multiple_of(i * TILE, TILE), TILE)
            restored = filter_tile(
                gath[c, :, cols], basis_ref[...], inverse_ref[...], power_ref[...]
            ).astype(jnp.bfloat16)
            filt[c, :, cols] = restored
            for p in range(n):
                at = p * frames
                edge[c, p, :, cols] = restored[at : at + STRIP].astype(jnp.float32)[0:1]
            return carry

        lax.fori_loop(0, columns // TILE, one, 0)
        row = c * n + me
        pltpu.make_async_copy(filt.at[c, span(me)], land.at[row], r2.at[c]).start()
        own_edge = edge.at[c, lax.rem(me + 1, n)]
        pltpu.make_async_copy(own_edge, after.at[row], r3.at[c]).start()
        for d in range(1, n):
            peer = lax.rem(me + d, n)
            to_peer(filt.at[c, span(peer)], land.at[row], s2.at[c], r2.at[c], peer).start()
            src = edge.at[c, lax.rem(peer + 1, n)]
            to_peer(src, after.at[row], s3.at[c], r3.at[c], peer).start()
        return carry

    lax.fori_loop(0, chunks, work, 0)

    lane = lax.broadcasted_iota(jnp.int32, (STRIP, columns), 1)
    frame = lax.broadcasted_iota(jnp.int32, (STRIP, columns), 0)
    at_low, at_high, at_last = lane == 0, lane == columns - 1, frame == STRIP - 1
    quarter = (2 * side - 1).astype(jnp.float32) * 0.25

    def left(x):
        return jnp.where(at_low, 0.0, pltpu.roll(x, 1, 1))

    def right(x):
        return jnp.where(at_high, 0.0, pltpu.roll(x, columns - 1, 1))

    def iterate(b, u_prev, v_prev, low, here, high):
        def mean(ref):
            center = ref[b, here]
            return 0.25 * (ref[b, low] + ref[b, high] + left(center) + right(center))

        mean_u, mean_v = mean(u_prev), mean(v_prev)
        gx, gy = gx_r[b, here], gy_r[b, here]
        common = (gx * mean_u + gy * mean_v + gt_r[b, here]) * inv_r[b, here]
        return mean_u - gx * common, mean_v - gy * common

    def step(b, e, first, second, outside=False):
        k0, k1, k2, k3 = (lax.rem(e + RING - back, RING) for back in range(4))
        total[b, k0] = first + second
        shift[b, k0] = second - first
        center = total[b, k1]
        gx = 0.25 * (right(center) - left(center))
        gy = quarter * (total[b, k0] - total[b, k2])
        gt = shift[b, k1]
        inv = 1.0 / (1.0 + gx * gx + gy * gy)
        common = gt * inv
        gx_r[b, k1], gy_r[b, k1], gt_r[b, k1], inv_r[b, k1] = gx, gy, gt, inv
        u1_r[b, k1] = -gx * common
        v1_r[b, k1] = -gy * common
        u2, v2 = iterate(b, u1_r, v1_r, k3, k2, k1)
        if outside:
            u2, v2 = jnp.zeros_like(u2), jnp.zeros_like(v2)
        u2_r[b, k2], v2_r[b, k2] = u2, v2
        u3, v3 = iterate(b, u2_r, v2_r, k0, k3, k2)
        q = jnp.maximum(e - 6, 0)
        start = lax.rem(q, n) * frames + b * STRIP
        place = pl.ds(pl.multiple_of(start, STRIP), STRIP)
        gath[q // n, place, :] = u3.astype(jnp.bfloat16)
        filt[q // n, place, :] = v3.astype(jnp.bfloat16)

    def pair(b, ref, after_ref, row):
        first = ref[row, pl.ds(pl.multiple_of(b * STRIP, STRIP), STRIP), :].astype(jnp.float32)
        later = jnp.minimum(b + 1, strips - 1)
        later = pl.ds(pl.multiple_of(later * STRIP, STRIP), STRIP)
        inside = ref[row, later, :].astype(jnp.float32)[0:1]
        upcoming = jnp.where(b == strips - 1, after_ref[row], inside)
        second = jnp.where(at_last, upcoming, pltpu.roll(first, STRIP - 1, 0))
        return first, second

    def emit(q):
        def send(src, dst, sem):
            block = src.at[q // n, span(lax.rem(q, n))]
            pltpu.make_async_copy(block, dst.at[physical(q)], sem).start()

        send(gath, u_ref, so.at[0])
        send(filt, v_ref, so.at[1])

    def arrive(c):
        pltpu.make_async_copy(filt.at[c], filt.at[c], r2.at[c]).wait()
        landed = after.at[pl.ds(c * n, n)]
        pltpu.make_async_copy(landed, landed, r3.at[c]).wait()
        sent = filt.at[c, pl.ds(0, (n - 1) * frames)]
        pltpu.make_async_copy(sent, sent, s2.at[c]).wait()

    def to_side(src, dst, k):
        return pltpu.make_async_remote_copy(
            src_ref=src,
            dst_ref=dst,
            send_sem=sh.at[k],
            recv_sem=rh.at[k],
            device_id={"space": 1 - side},
            device_id_type=MESH,
        )

    arrive(0)
    halo = (
        to_side(land.at[pl.ds(0, 3)], land_h, 0),
        to_side(after.at[pl.ds(0, 3)], after_h, 1),
    )
    for copy in halo:
        copy.start()
    for copy in halo:
        copy.wait()

    def group(g, carry):
        @pl.when(g > 0)
        def _():
            arrive(g)

        def strip(b, carry):
            @pl.when(g == 0)
            def _():
                def before(e, carry):
                    step(b, e, *pair(b, land_h, after_h, 2 - e))
                    return carry

                lax.fori_loop(0, 3, before, 0)

            def inner(i, carry):
                row = g * n + i
                step(b, row + 3, *pair(b, land, after, row))
                return carry

            lax.fori_loop(0, n, inner, 0)
            return carry

        lax.fori_loop(0, strips, strip, 0)

        def out(i, carry):
            q = g * n - 3 + i

            @pl.when(q >= 0)
            def _():
                emit(q)

            return carry

        lax.fori_loop(0, n, out, 0)
        return carry

    lax.fori_loop(0, chunks, group, 0)

    def finish(b, carry):
        zero = jnp.zeros((STRIP, columns), jnp.float32)
        for i in range(3):
            step(b, rows + 3 + i, zero, zero, outside=i == 2)
        return carry

    lax.fori_loop(0, strips, finish, 0)
    for i in range(3):
        emit(rows - 3 + i)

    def drain(c, carry):
        sent = filt.at[c, pl.ds(0, (n - 1) * frames)]
        pltpu.make_async_copy(sent, sent, s1.at[c]).wait()
        sent = after.at[pl.ds(0, n - 1)]
        pltpu.make_async_copy(sent, sent, s3.at[c]).wait()
        return carry

    lax.fori_loop(0, chunks, drain, 0)
    pltpu.make_async_copy(u_ref, u_ref, so.at[0]).wait()
    pltpu.make_async_copy(v_ref, v_ref, so.at[1]).wait()


def exchange_and_flow(frames, signal_power):
    n = lax.axis_size("tm")
    count, rows, columns = frames.shape
    chunks, half, strips = rows // n, F // 2, count // STRIP
    basis, inverse = real_basis()
    power = jnp.concatenate([signal_power, signal_power[1:half]], axis=0)
    power = jnp.broadcast_to(power[:, None], (F, TILE))
    vmem = pl.BlockSpec(memory_space=pltpu.VMEM)
    hbm = pl.BlockSpec(memory_space=pl.ANY)
    out = jax.ShapeDtypeStruct((rows, count, columns), jnp.bfloat16)
    dma = pltpu.SemaphoreType.DMA
    return pl.pallas_call(
        functools.partial(fused_kernel, n),
        out_shape=(out, out),
        in_specs=[hbm, vmem, vmem, vmem],
        out_specs=(hbm, hbm),
        scratch_shapes=[
            pltpu.VMEM((2, count, STRIP, columns), jnp.bfloat16),
            pltpu.VMEM((rows, count, columns), jnp.bfloat16),
            pltpu.VMEM((chunks, F, columns), jnp.bfloat16),
            pltpu.VMEM((chunks, F, columns), jnp.bfloat16),
            pltpu.VMEM((rows, count, columns), jnp.bfloat16),
            pltpu.VMEM((chunks, n, 1, columns), jnp.float32),
            pltpu.VMEM((rows, 1, columns), jnp.float32),
            pltpu.VMEM((3, count, columns), jnp.bfloat16),
            pltpu.VMEM((3, 1, columns), jnp.float32),
        ]
        + [pltpu.VMEM((strips, RING, STRIP, columns), jnp.float32)] * 10
        + [dma((2,))]
        + [dma((chunks,))] * 6
        + [dma((2,))] * 3,
        compiler_params=pltpu.CompilerParams(
            collective_id=0, has_side_effects=True, vmem_limit_bytes=60 * 2**20
        ),
        cost_estimate=pl.CostEstimate(
            flops=4 * F * rows * count * columns,
            bytes_accessed=6 * rows * count * columns,
            transcendentals=0,
        ),
        name="exchange",
    )(frames, jnp.asarray(basis), jnp.asarray(inverse), power)


def widen_kernel(u_in, v_in, u_out, v_out):
    for b in range(0, u_in.shape[2], TILE):
        cols = slice(b, b + TILE)
        u_out[:, :, cols] = jnp.swapaxes(u_in[:, :, cols].astype(jnp.float32), 0, 1)
        v_out[:, :, cols] = jnp.swapaxes(v_in[:, :, cols].astype(jnp.float32), 0, 1)


def widen(u, v):
    rows, count, columns = u.shape
    out = jax.ShapeDtypeStruct((count, rows, columns), jnp.float32)
    in_spec = pl.BlockSpec((STRIP, STRIP, columns), lambda i, j: (j, i, 0))
    out_spec = pl.BlockSpec((STRIP, STRIP, columns), lambda i, j: (i, j, 0))
    return pl.pallas_call(
        widen_kernel,
        grid=(count // STRIP, rows // STRIP),
        out_shape=(out, out),
        in_specs=[in_spec, in_spec],
        out_specs=(out_spec, out_spec),
        compiler_params=pltpu.CompilerParams(vmem_limit_bytes=40 * 2**20),
        cost_estimate=pl.CostEstimate(
            flops=0, bytes_accessed=12 * rows * count * columns, transcendentals=0
        ),
        name="widen",
    )(u, v)


def shards(frames, signal_power):
    n = lax.axis_size("tm")
    count, rows, columns = frames.shape
    fits = n >= 3 and count % STRIP == 0 and rows % (2 * STRIP) == 0 and rows % n == 0
    fits = fits and STRIP % n == 0 and columns % TILE == 0 and lax.axis_size("space") == 2
    if not fits:
        return plain_shards(frames, signal_power)
    return widen(*exchange_and_flow(frames, signal_power))


def solution(mesh):
    in_specs = (P("tm", ("band", "space"), None), P())
    out_specs = (P("tm", ("band", "space"), None), P("tm", ("band", "space"), None))
    return jax.shard_map(shards, mesh=mesh, in_specs=in_specs, out_specs=out_specs, check_vma=False)
```

```python
import functools
import math

import jax
import jax.numpy as jnp
import numpy as np
from jax import lax
from jax.experimental import pallas as pl
from jax.experimental.pallas import tpu as pltpu
from jax.sharding import PartitionSpec as P

F = 512
ITERS = 3


def from_behind(block, axis, distance):
    devices = range(lax.axis_size(axis))
    route = [((i - distance) % len(devices), i) for i in devices]
    return lax.ppermute(block, axis, route)


def padded_2(block, sides, width):
    for axis, dim in sides:
        count = lax.axis_size(axis)
        forward = [(i, i + 1) for i in range(count - 1)]
        backward = [(target, source) for source, target in forward]
        low = lax.ppermute(
            lax.slice_in_dim(block, block.shape[dim] - width, None, axis=dim), axis, forward
        )
        high = lax.ppermute(lax.slice_in_dim(block, 0, width, axis=dim), axis, backward)
        block = jnp.concatenate([low, block, high], axis=dim)
    return block


def make_tables():
    freq = jnp.arange(F, dtype=jnp.int32)
    phase = freq[:, None] * freq[None, :] % F
    angle = phase.astype(jnp.float32) * (2.0 * math.pi / F)
    return (jnp.cos(angle).astype(jnp.bfloat16), jnp.sin(angle).astype(jnp.bfloat16))


def full_power(signal_power):
    return jnp.concatenate([signal_power, signal_power[1 : F // 2][::-1]], axis=0)


def wiener_block(block, cosines, sines, power_full):
    real_part = jnp.dot(cosines, block, preferred_element_type=jnp.float32)
    imag_part = jnp.dot(sines, block, preferred_element_type=jnp.float32)
    energy = real_part * real_part + imag_part * imag_part
    noise = jnp.mean(energy[F // 4 : 3 * F // 4], axis=0) / F + 1e-06
    weight = power_full[:, None] / (power_full[:, None] + noise[None, :])
    scaled_real = (weight * real_part).astype(jnp.bfloat16)
    scaled_imag = (weight * imag_part).astype(jnp.bfloat16)
    restored = jnp.dot(cosines, scaled_real, preferred_element_type=jnp.float32)
    restored = restored + jnp.dot(sines, scaled_imag, preferred_element_type=jnp.float32)
    return (restored / F).astype(jnp.bfloat16)


def across_columns(field):
    padded = jnp.pad(field, ((0, 0), (0, 0), (1, 1)))
    return padded[:, :, 2:] - padded[:, :, :-2]


def vertical_mean(extended):
    center = extended[:, 1:-1, :]
    col_pad = jnp.pad(center, ((0, 0), (0, 0), (1, 1)))
    return 0.25 * (
        extended[:, :-2, :] + extended[:, 2:, :] + col_pad[:, :, :-2] + col_pad[:, :, 2:]
    )


def derivatives(extended_pair):
    first = extended_pair[0].astype(jnp.float32)
    second = extended_pair[1].astype(jnp.float32)
    first_mid = first[:, 1:-1, :]
    second_mid = second[:, 1:-1, :]
    grad_x = 0.25 * (across_columns(first_mid) + across_columns(second_mid))
    grad_y = 0.25 * (first[:, 2:, :] - first[:, :-2, :] + (second[:, 2:, :] - second[:, :-2, :]))
    grad_t = second_mid - first_mid
    denom = 1.0 + grad_x * grad_x + grad_y * grad_y
    return (grad_x, grad_y, grad_t, denom)


def plain_shards(frames, signal_power):
    cosines, sines = make_tables()
    power_full = full_power(signal_power)
    gathered = lax.all_to_all(frames, "tm", split_axis=1, concat_axis=0, tiled=True)
    shape_now = gathered.shape
    flat = gathered.reshape(shape_now[0], shape_now[1] * shape_now[2])
    restored = lax.all_to_all(
        wiener_block(flat, cosines, sines, power_full).reshape(shape_now),
        "tm",
        split_axis=0,
        concat_axis=1,
        tiled=True,
    )
    following = from_behind(restored[0], "tm", -1)
    upcoming = jnp.concatenate([restored[1:], following[None]], axis=0)
    frame_pair = jnp.stack([restored, upcoming], axis=0)
    extended_pair = padded_2(frame_pair, (("space", 2),), 1)
    grad_x, grad_y, grad_t, denom = derivatives(extended_pair)
    flow_u = jnp.zeros_like(grad_x)
    flow_v = jnp.zeros_like(grad_x)
    for iteration in range(ITERS):
        if iteration == 0:
            mean_u = vertical_mean(jnp.pad(flow_u, ((0, 0), (1, 1), (0, 0))))
            mean_v = vertical_mean(jnp.pad(flow_v, ((0, 0), (1, 1), (0, 0))))
        else:
            extended_flow = padded_2(jnp.stack([flow_u, flow_v], axis=0), (("space", 2),), 1)
            mean_u = vertical_mean(extended_flow[0])
            mean_v = vertical_mean(extended_flow[1])
        common = (grad_x * mean_u + grad_y * mean_v + grad_t) / denom
        flow_u = mean_u - grad_x * common
        flow_v = mean_v - grad_y * common
    return (flow_u, flow_v)


MESH = pl.DeviceIdType.MESH


def real_basis():
    freq = np.arange(F)
    angle = (freq[:, None] * freq[None, :] % F).astype(np.float32) * np.float32(2.0 * math.pi / F)
    half = F // 2
    basis = np.concatenate(
        [np.cos(angle[:half]), np.cos(angle[half : half + 1]), np.sin(angle[1:half])], axis=0
    ).astype(jnp.bfloat16)
    weight = np.full((F,), 2.0 / F, np.float32)
    weight[0] = weight[half] = 1.0 / F
    inverse = (basis.astype(np.float32) * weight[:, None]).T.astype(jnp.bfloat16)
    return basis, np.ascontiguousarray(inverse)


STRIP = 16
RING = 4
TILE = 256
DELAY = 2


def filter_tile(block, basis, inverse, power):
    half, quarter = F // 2, F // 4
    spectrum = jnp.dot(basis, block, preferred_element_type=jnp.float32)
    energy = spectrum * spectrum
    upper = energy[quarter:half] + energy[half + quarter :]
    total = 2.0 * jnp.sum(upper, axis=0, keepdims=True) - upper[0:1] + energy[half : half + 1]
    noise = total * (1.0 / (half * F)) + 1e-06
    scaled = (power / (power + noise) * spectrum).astype(jnp.bfloat16)
    return jnp.dot(inverse, scaled, preferred_element_type=jnp.float32)


def fused_kernel(n, x_ref, basis_ref, inverse_ref, power_ref, u_ref, v_ref, *scratch):
    (xin, xt, gath, filt, land, edge, after, land_h, after_h) = scratch[:9]
    (total, shift, gx_r, gy_r, gt_r, inv_r, u1_r, v1_r, u2_r, v2_r) = scratch[9:19]
    (sx, s1, r1, s2, r2, s3, r3, sh, rh, so) = scratch[19:]
    me, side = lax.axis_index("tm"), lax.axis_index("space")
    frames, rows, columns = x_ref.shape
    chunks, blocks, strips = rows // n, rows // STRIP, frames // STRIP
    per_block = chunks // blocks

    def physical(row):
        return side * row + (1 - side) * (rows - 1 - row)

    def block_rows(m):
        first = side * m + (1 - side) * (blocks - 1 - m)
        return pl.ds(pl.multiple_of(first * STRIP, STRIP), STRIP)

    def span(device):
        return pl.ds(pl.multiple_of(device * frames, frames), frames)

    def fetch(m):
        slot = lax.rem(m, 2)
        return pltpu.make_async_copy(x_ref.at[:, block_rows(m), :], xin.at[slot], sx.at[slot])

    fetch(0).start()
    fetch(1).start()
    barrier = pltpu.get_barrier_semaphore()
    for d in range(1, n):
        peer = lax.rem(me + d, n)
        pl.semaphore_signal(barrier, inc=1, device_id={"tm": peer}, device_id_type=MESH)
    pl.semaphore_signal(barrier, inc=1, device_id={"space": 1 - side}, device_id_type=MESH)
    pl.semaphore_wait(barrier, n)

    def to_peer(src, dst, send, recv, peer):
        return pltpu.make_async_remote_copy(
            src_ref=src,
            dst_ref=dst,
            send_sem=send,
            recv_sem=recv,
            device_id={"tm": peer},
            device_id_type=MESH,
        )

    def scatter(m, carry):
        fetch(m).wait()
        slot = lax.rem(m, 2)
        per_row = columns // TILE

        def turn(i, carry):
            cols = pl.ds(pl.multiple_of(lax.rem(i, per_row) * TILE, TILE), TILE)
            part = pl.ds(pl.multiple_of(i // per_row * STRIP, STRIP), STRIP)
            piece = xin[slot, part, :, cols].astype(jnp.float32)
            xt[block_rows(m), part, cols] = jnp.swapaxes(piece, 0, 1).astype(jnp.bfloat16)
            return carry

        lax.fori_loop(0, strips * per_row, turn, 0)

        @pl.when(m + 2 < blocks)
        def _():
            fetch(m + 2).start()

        for k in range(per_block):
            c = m * per_block + k
            own = xt.at[physical(c * n + me)]
            pltpu.make_async_copy(own, gath.at[c, span(me)], r1.at[c]).start()
            for d in range(1, n):
                peer = lax.rem(me + d, n)
                src = xt.at[physical(c * n + peer)]
                to_peer(src, gath.at[c, span(me)], s1.at[c], r1.at[c], peer).start()
        return carry

    lax.fori_loop(0, blocks, scatter, 0)

    def work(c):
        pltpu.make_async_copy(gath.at[c], gath.at[c], r1.at[c]).wait()

        def one(i, carry):
            cols = pl.ds(pl.multiple_of(i * TILE, TILE), TILE)
            restored = filter_tile(
                gath[c, :, cols], basis_ref[...], inverse_ref[...], power_ref[...]
            ).astype(jnp.bfloat16)
            filt[c, :, cols] = restored
            for p in range(n):
                at = p * frames
                edge[c, p, :, cols] = restored[at : at + STRIP].astype(jnp.float32)[0:1]
            return carry

        lax.fori_loop(0, columns // TILE, one, 0)
        row = c * n + me
        pltpu.make_async_copy(filt.at[c, span(me)], land.at[row], r2.at[c]).start()
        own_edge = edge.at[c, lax.rem(me + 1, n)]
        pltpu.make_async_copy(own_edge, after.at[row], r3.at[c]).start()
        for d in range(1, n):
            peer = lax.rem(me + d, n)
            to_peer(filt.at[c, span(peer)], land.at[row], s2.at[c], r2.at[c], peer).start()
            src = edge.at[c, lax.rem(peer + 1, n)]
            to_peer(src, after.at[row], s3.at[c], r3.at[c], peer).start()

    lane = lax.broadcasted_iota(jnp.int32, (STRIP, 128), 1)
    frame = lax.broadcasted_iota(jnp.int32, (STRIP, columns), 0)
    at_low, at_high, at_last = lane == 0, lane == 127, frame == STRIP - 1
    quarter = (2 * side - 1).astype(jnp.float32) * 0.25

    def left(x):
        turned = pltpu.roll(x, 1, 1)
        return jnp.concatenate(
            [jnp.where(at_low, 0.0, turned[:, :128]), turned[:, 128:]], axis=1
        )

    def right(x):
        turned = pltpu.roll(x, columns - 1, 1)
        return jnp.concatenate(
            [turned[:, :-128], jnp.where(at_high, 0.0, turned[:, -128:])], axis=1
        )

    def iterate(b, u_prev, v_prev, low, here, high):
        def mean(ref):
            center = ref[b, here]
            return 0.25 * (ref[b, low] + ref[b, high] + left(center) + right(center))

        mean_u, mean_v = mean(u_prev), mean(v_prev)
        gx, gy = gx_r[b, here], gy_r[b, here]
        common = (gx * mean_u + gy * mean_v + gt_r[b, here]) * inv_r[b, here]
        return mean_u - gx * common, mean_v - gy * common

    def step(b, e, first, second, outside=False):
        k0, k1, k2, k3 = (lax.rem(e + RING - back, RING) for back in range(4))
        total[b, k0] = first + second
        shift[b, k0] = second - first
        center = total[b, k1]
        gx = 0.25 * (right(center) - left(center))
        gy = quarter * (total[b, k0] - total[b, k2])
        gt = shift[b, k1]
        inv = 1.0 / (1.0 + gx * gx + gy * gy)
        common = gt * inv
        gx_r[b, k1], gy_r[b, k1], gt_r[b, k1], inv_r[b, k1] = gx, gy, gt, inv
        u1_r[b, k1] = -gx * common
        v1_r[b, k1] = -gy * common
        u2, v2 = iterate(b, u1_r, v1_r, k3, k2, k1)
        if outside:
            u2, v2 = jnp.zeros_like(u2), jnp.zeros_like(v2)
        u2_r[b, k2], v2_r[b, k2] = u2, v2
        u3, v3 = iterate(b, u2_r, v2_r, k0, k3, k2)
        q = jnp.maximum(e - 6, 0)
        start = lax.rem(q, n) * frames + b * STRIP
        place = pl.ds(pl.multiple_of(start, STRIP), STRIP)
        gath[q // n, place, :] = u3.astype(jnp.bfloat16)
        filt[q // n, place, :] = v3.astype(jnp.bfloat16)

    def pair(b, ref, after_ref, row):
        first = ref[row, pl.ds(pl.multiple_of(b * STRIP, STRIP), STRIP), :].astype(jnp.float32)
        later = jnp.minimum(b + 1, strips - 1)
        later = pl.ds(pl.multiple_of(later * STRIP, STRIP), STRIP)
        inside = ref[row, later, :].astype(jnp.float32)[0:1]
        upcoming = jnp.where(b == strips - 1, after_ref[row], inside)
        second = jnp.where(at_last, upcoming, pltpu.roll(first, STRIP - 1, 0))
        return first, second

    def emit(q):
        def send(src, dst, sem):
            block = src.at[q // n, span(lax.rem(q, n))]
            pltpu.make_async_copy(block, dst.at[physical(q)], sem).start()

        send(gath, u_ref, so.at[0])
        send(filt, v_ref, so.at[1])

    def arrive(c):
        pltpu.make_async_copy(filt.at[c], filt.at[c], r2.at[c]).wait()
        landed = after.at[pl.ds(c * n, n)]
        pltpu.make_async_copy(landed, landed, r3.at[c]).wait()
        sent = filt.at[c, pl.ds(0, (n - 1) * frames)]
        pltpu.make_async_copy(sent, sent, s2.at[c]).wait()

    def to_side(src, dst, k):
        return pltpu.make_async_remote_copy(
            src_ref=src,
            dst_ref=dst,
            send_sem=sh.at[k],
            recv_sem=rh.at[k],
            device_id={"space": 1 - side},
            device_id_type=MESH,
        )

    def group(g):
        arrive(g)

        @pl.when(g == 0)
        def _():
            halo = (
                to_side(land.at[pl.ds(0, 3)], land_h, 0),
                to_side(after.at[pl.ds(0, 3)], after_h, 1),
            )
            for copy in halo:
                copy.start()
            for copy in halo:
                copy.wait()

        def strip(b, carry):
            @pl.when(g == 0)
            def _():
                def before(e, carry):
                    step(b, e, *pair(b, land_h, after_h, 2 - e))
                    return carry

                lax.fori_loop(0, 3, before, 0)

            def inner(i, carry):
                row = g * n + i
                step(b, row + 3, *pair(b, land, after, row))
                return carry

            lax.fori_loop(0, n, inner, 0)
            return carry

        lax.fori_loop(0, strips, strip, 0)

        def out(i, carry):
            q = g * n - 3 + i

            @pl.when(q >= 0)
            def _():
                emit(q)

            return carry

        lax.fori_loop(0, n, out, 0)

    def turn_of(c, carry):
        @pl.when(c < chunks)
        def _():
            work(c)

        @pl.when(c >= DELAY)
        def _():
            group(c - DELAY)

        return carry

    lax.fori_loop(0, chunks + DELAY, turn_of, 0)

    def finish(b, carry):
        zero = jnp.zeros((STRIP, columns), jnp.float32)
        for i in range(3):
            step(b, rows + 3 + i, zero, zero, outside=i == 2)
        return carry

    lax.fori_loop(0, strips, finish, 0)
    for i in range(3):
        emit(rows - 3 + i)

    def drain(c, carry):
        sent = filt.at[c, pl.ds(0, (n - 1) * frames)]
        pltpu.make_async_copy(sent, sent, s1.at[c]).wait()
        sent = after.at[pl.ds(0, n - 1)]
        pltpu.make_async_copy(sent, sent, s3.at[c]).wait()
        return carry

    lax.fori_loop(0, chunks, drain, 0)
    pltpu.make_async_copy(u_ref, u_ref, so.at[0]).wait()
    pltpu.make_async_copy(v_ref, v_ref, so.at[1]).wait()


def exchange_and_flow(frames, signal_power):
    n = lax.axis_size("tm")
    count, rows, columns = frames.shape
    chunks, half, strips = rows // n, F // 2, count // STRIP
    basis, inverse = real_basis()
    power = jnp.concatenate([signal_power, signal_power[1:half]], axis=0)
    power = jnp.broadcast_to(power[:, None], (F, TILE))
    vmem = pl.BlockSpec(memory_space=pltpu.VMEM)
    hbm = pl.BlockSpec(memory_space=pl.ANY)
    out = jax.ShapeDtypeStruct((rows, count, columns), jnp.bfloat16)
    dma = pltpu.SemaphoreType.DMA
    return pl.pallas_call(
        functools.partial(fused_kernel, n),
        out_shape=(out, out),
        in_specs=[hbm, vmem, vmem, vmem],
        out_specs=(hbm, hbm),
        scratch_shapes=[
            pltpu.VMEM((2, count, STRIP, columns), jnp.bfloat16),
            pltpu.VMEM((rows, count, columns), jnp.bfloat16),
            pltpu.VMEM((chunks, F, columns), jnp.bfloat16),
            pltpu.VMEM((chunks, F, columns), jnp.bfloat16),
            pltpu.VMEM((rows, count, columns), jnp.bfloat16),
            pltpu.VMEM((chunks, n, 1, columns), jnp.float32),
            pltpu.VMEM((rows, 1, columns), jnp.float32),
            pltpu.VMEM((3, count, columns), jnp.bfloat16),
            pltpu.VMEM((3, 1, columns), jnp.float32),
        ]
        + [pltpu.VMEM((strips, RING, STRIP, columns), jnp.float32)] * 10
        + [dma((2,))]
        + [dma((chunks,))] * 6
        + [dma((2,))] * 3,
        compiler_params=pltpu.CompilerParams(
            collective_id=0, has_side_effects=True, vmem_limit_bytes=60 * 2**20
        ),
        cost_estimate=pl.CostEstimate(
            flops=4 * F * rows * count * columns,
            bytes_accessed=6 * rows * count * columns,
            transcendentals=0,
        ),
        name="exchange",
    )(frames, jnp.asarray(basis), jnp.asarray(inverse), power)


def widen_kernel(u_in, v_in, u_out, v_out):
    for b in range(0, u_in.shape[2], TILE):
        cols = slice(b, b + TILE)
        u_out[:, :, cols] = jnp.swapaxes(u_in[:, :, cols].astype(jnp.float32), 0, 1)
        v_out[:, :, cols] = jnp.swapaxes(v_in[:, :, cols].astype(jnp.float32), 0, 1)


def widen(u, v):
    rows, count, columns = u.shape
    out = jax.ShapeDtypeStruct((count, rows, columns), jnp.float32)
    in_spec = pl.BlockSpec((STRIP, STRIP, columns), lambda i, j: (j, i, 0))
    out_spec = pl.BlockSpec((STRIP, STRIP, columns), lambda i, j: (i, j, 0))
    return pl.pallas_call(
        widen_kernel,
        grid=(count // STRIP, rows // STRIP),
        out_shape=(out, out),
        in_specs=[in_spec, in_spec],
        out_specs=(out_spec, out_spec),
        compiler_params=pltpu.CompilerParams(vmem_limit_bytes=60 * 2**20),
        cost_estimate=pl.CostEstimate(
            flops=0, bytes_accessed=12 * rows * count * columns, transcendentals=0
        ),
        name="widen",
    )(u, v)


def shards(frames, signal_power):
    n = lax.axis_size("tm")
    count, rows, columns = frames.shape
    fits = n >= 3 and count % STRIP == 0 and rows % (2 * STRIP) == 0 and rows % n == 0
    fits = fits and STRIP % n == 0 and columns % TILE == 0 and lax.axis_size("space") == 2
    if not fits:
        return plain_shards(frames, signal_power)
    return widen(*exchange_and_flow(frames, signal_power))


def solution(mesh):
    in_specs = (P("tm", ("band", "space"), None), P())
    out_specs = (P("tm", ("band", "space"), None), P("tm", ("band", "space"), None))
    return jax.shard_map(shards, mesh=mesh, in_specs=in_specs, out_specs=out_specs, check_vma=False)
```

```python
import functools
import math

import jax
import jax.numpy as jnp
import numpy as np
from jax import lax
from jax.experimental import pallas as pl
from jax.experimental.pallas import tpu as pltpu
from jax.sharding import PartitionSpec as P

F = 512
ITERS = 3


def from_behind(block, axis, distance):
    devices = range(lax.axis_size(axis))
    route = [((i - distance) % len(devices), i) for i in devices]
    return lax.ppermute(block, axis, route)


def padded_2(block, sides, width):
    for axis, dim in sides:
        count = lax.axis_size(axis)
        forward = [(i, i + 1) for i in range(count - 1)]
        backward = [(target, source) for source, target in forward]
        low = lax.ppermute(
            lax.slice_in_dim(block, block.shape[dim] - width, None, axis=dim), axis, forward
        )
        high = lax.ppermute(lax.slice_in_dim(block, 0, width, axis=dim), axis, backward)
        block = jnp.concatenate([low, block, high], axis=dim)
    return block


def make_tables():
    freq = jnp.arange(F, dtype=jnp.int32)
    phase = freq[:, None] * freq[None, :] % F
    angle = phase.astype(jnp.float32) * (2.0 * math.pi / F)
    return (jnp.cos(angle).astype(jnp.bfloat16), jnp.sin(angle).astype(jnp.bfloat16))


def full_power(signal_power):
    return jnp.concatenate([signal_power, signal_power[1 : F // 2][::-1]], axis=0)


def wiener_block(block, cosines, sines, power_full):
    real_part = jnp.dot(cosines, block, preferred_element_type=jnp.float32)
    imag_part = jnp.dot(sines, block, preferred_element_type=jnp.float32)
    energy = real_part * real_part + imag_part * imag_part
    noise = jnp.mean(energy[F // 4 : 3 * F // 4], axis=0) / F + 1e-06
    weight = power_full[:, None] / (power_full[:, None] + noise[None, :])
    scaled_real = (weight * real_part).astype(jnp.bfloat16)
    scaled_imag = (weight * imag_part).astype(jnp.bfloat16)
    restored = jnp.dot(cosines, scaled_real, preferred_element_type=jnp.float32)
    restored = restored + jnp.dot(sines, scaled_imag, preferred_element_type=jnp.float32)
    return (restored / F).astype(jnp.bfloat16)


def across_columns(field):
    padded = jnp.pad(field, ((0, 0), (0, 0), (1, 1)))
    return padded[:, :, 2:] - padded[:, :, :-2]


def vertical_mean(extended):
    center = extended[:, 1:-1, :]
    col_pad = jnp.pad(center, ((0, 0), (0, 0), (1, 1)))
    return 0.25 * (
        extended[:, :-2, :] + extended[:, 2:, :] + col_pad[:, :, :-2] + col_pad[:, :, 2:]
    )


def derivatives(extended_pair):
    first = extended_pair[0].astype(jnp.float32)
    second = extended_pair[1].astype(jnp.float32)
    first_mid = first[:, 1:-1, :]
    second_mid = second[:, 1:-1, :]
    grad_x = 0.25 * (across_columns(first_mid) + across_columns(second_mid))
    grad_y = 0.25 * (first[:, 2:, :] - first[:, :-2, :] + (second[:, 2:, :] - second[:, :-2, :]))
    grad_t = second_mid - first_mid
    denom = 1.0 + grad_x * grad_x + grad_y * grad_y
    return (grad_x, grad_y, grad_t, denom)


def plain_shards(frames, signal_power):
    cosines, sines = make_tables()
    power_full = full_power(signal_power)
    gathered = lax.all_to_all(frames, "tm", split_axis=1, concat_axis=0, tiled=True)
    shape_now = gathered.shape
    flat = gathered.reshape(shape_now[0], shape_now[1] * shape_now[2])
    restored = lax.all_to_all(
        wiener_block(flat, cosines, sines, power_full).reshape(shape_now),
        "tm",
        split_axis=0,
        concat_axis=1,
        tiled=True,
    )
    following = from_behind(restored[0], "tm", -1)
    upcoming = jnp.concatenate([restored[1:], following[None]], axis=0)
    frame_pair = jnp.stack([restored, upcoming], axis=0)
    extended_pair = padded_2(frame_pair, (("space", 2),), 1)
    grad_x, grad_y, grad_t, denom = derivatives(extended_pair)
    flow_u = jnp.zeros_like(grad_x)
    flow_v = jnp.zeros_like(grad_x)
    for iteration in range(ITERS):
        if iteration == 0:
            mean_u = vertical_mean(jnp.pad(flow_u, ((0, 0), (1, 1), (0, 0))))
            mean_v = vertical_mean(jnp.pad(flow_v, ((0, 0), (1, 1), (0, 0))))
        else:
            extended_flow = padded_2(jnp.stack([flow_u, flow_v], axis=0), (("space", 2),), 1)
            mean_u = vertical_mean(extended_flow[0])
            mean_v = vertical_mean(extended_flow[1])
        common = (grad_x * mean_u + grad_y * mean_v + grad_t) / denom
        flow_u = mean_u - grad_x * common
        flow_v = mean_v - grad_y * common
    return (flow_u, flow_v)


MESH = pl.DeviceIdType.MESH


def real_basis():
    freq = np.arange(F)
    angle = (freq[:, None] * freq[None, :] % F).astype(np.float32) * np.float32(2.0 * math.pi / F)
    half = F // 2
    basis = np.concatenate(
        [np.cos(angle[:half]), np.cos(angle[half : half + 1]), np.sin(angle[1:half])], axis=0
    ).astype(jnp.bfloat16)
    weight = np.full((F,), 2.0 / F, np.float32)
    weight[0] = weight[half] = 1.0 / F
    inverse = (basis.astype(np.float32) * weight[:, None]).T.astype(jnp.bfloat16)
    return basis, np.ascontiguousarray(inverse)


STRIP = 16
RING = 4
TILE = 256
DELAY = 2


def filter_tile(block, basis, inverse, power):
    half, quarter = F // 2, F // 4
    spectrum = jnp.dot(basis, block, preferred_element_type=jnp.float32)
    energy = spectrum * spectrum
    upper = energy[quarter:half] + energy[half + quarter :]
    total = 2.0 * jnp.sum(upper, axis=0, keepdims=True) - upper[0:1] + energy[half : half + 1]
    noise = total * (1.0 / (half * F)) + 1e-06
    scaled = (power / (power + noise) * spectrum).astype(jnp.bfloat16)
    return jnp.dot(inverse, scaled, preferred_element_type=jnp.float32)


def fused_kernel(n, x_ref, basis_ref, inverse_ref, power_ref, u_ref, v_ref, *scratch):
    (xin, xt, gath, filt, land, edge, after, land_h, after_h) = scratch[:9]
    (total, shift, gx_r, gy_r, gt_r, inv_r, u1_r, v1_r, u2_r, v2_r) = scratch[9:19]
    (sx, s1, r1, s2, r2, s3, r3, sh, rh, so) = scratch[19:]
    me, side = lax.axis_index("tm"), lax.axis_index("space")
    frames, rows, columns = x_ref.shape
    chunks, blocks, strips = rows // n, rows // STRIP, frames // STRIP
    per_block = chunks // blocks

    def physical(row):
        return side * row + (1 - side) * (rows - 1 - row)

    def block_rows(m):
        first = side * m + (1 - side) * (blocks - 1 - m)
        return pl.ds(pl.multiple_of(first * STRIP, STRIP), STRIP)

    def span(device):
        return pl.ds(pl.multiple_of(device * frames, frames), frames)

    def fetch(m):
        slot = lax.rem(m, 2)
        return pltpu.make_async_copy(x_ref.at[:, block_rows(m), :], xin.at[slot], sx.at[slot])

    fetch(0).start()
    fetch(1).start()
    barrier = pltpu.get_barrier_semaphore()
    for d in range(1, n):
        peer = lax.rem(me + d, n)
        pl.semaphore_signal(barrier, inc=1, device_id={"tm": peer}, device_id_type=MESH)
    pl.semaphore_signal(barrier, inc=1, device_id={"space": 1 - side}, device_id_type=MESH)
    pl.semaphore_wait(barrier, n)

    def to_peer(src, dst, send, recv, peer):
        return pltpu.make_async_remote_copy(
            src_ref=src,
            dst_ref=dst,
            send_sem=send,
            recv_sem=recv,
            device_id={"tm": peer},
            device_id_type=MESH,
        )

    def scatter(m):
        fetch(m).wait()
        slot = lax.rem(m, 2)
        per_row = columns // TILE

        def turn(i, carry):
            cols = pl.ds(pl.multiple_of(lax.rem(i, per_row) * TILE, TILE), TILE)
            part = pl.ds(pl.multiple_of(i // per_row * STRIP, STRIP), STRIP)
            piece = xin[slot, part, :, cols].astype(jnp.float32)
            xt[block_rows(m), part, cols] = jnp.swapaxes(piece, 0, 1).astype(jnp.bfloat16)
            return carry

        lax.fori_loop(0, strips * per_row, turn, 0)

        @pl.when(m + 2 < blocks)
        def _():
            fetch(m + 2).start()

        for k in range(per_block):
            c = m * per_block + k
            own = xt.at[physical(c * n + me)]
            pltpu.make_async_copy(own, gath.at[c, span(me)], r1.at[c]).start()
            for d in range(1, n):
                peer = lax.rem(me + d, n)
                src = xt.at[physical(c * n + peer)]
                to_peer(src, gath.at[c, span(me)], s1.at[c], r1.at[c], peer).start()

    def work(c):
        pltpu.make_async_copy(gath.at[c], gath.at[c], r1.at[c]).wait()

        def one(i, carry):
            cols = pl.ds(pl.multiple_of(i * TILE, TILE), TILE)
            restored = filter_tile(
                gath[c, :, cols], basis_ref[...], inverse_ref[...], power_ref[...]
            ).astype(jnp.bfloat16)
            filt[c, :, cols] = restored
            for p in range(n):
                at = p * frames
                edge[c, p, :, cols] = restored[at : at + STRIP].astype(jnp.float32)[0:1]
            return carry

        lax.fori_loop(0, columns // TILE, one, 0)
        row = c * n + me
        pltpu.make_async_copy(filt.at[c, span(me)], land.at[row], r2.at[c]).start()
        own_edge = edge.at[c, lax.rem(me + 1, n)]
        pltpu.make_async_copy(own_edge, after.at[row], r3.at[c]).start()
        for d in range(1, n):
            peer = lax.rem(me + d, n)
            to_peer(filt.at[c, span(peer)], land.at[row], s2.at[c], r2.at[c], peer).start()
            src = edge.at[c, lax.rem(peer + 1, n)]
            to_peer(src, after.at[row], s3.at[c], r3.at[c], peer).start()

    lane = lax.broadcasted_iota(jnp.int32, (STRIP, 128), 1)
    frame = lax.broadcasted_iota(jnp.int32, (STRIP, columns), 0)
    at_low, at_high, at_last = lane == 0, lane == 127, frame == STRIP - 1
    quarter = (2 * side - 1).astype(jnp.float32) * 0.25

    def left(x):
        turned = pltpu.roll(x, 1, 1)
        return jnp.concatenate(
            [jnp.where(at_low, 0.0, turned[:, :128]), turned[:, 128:]], axis=1
        )

    def right(x):
        turned = pltpu.roll(x, columns - 1, 1)
        return jnp.concatenate(
            [turned[:, :-128], jnp.where(at_high, 0.0, turned[:, -128:])], axis=1
        )

    def iterate(b, u_prev, v_prev, low, here, high):
        def mean(ref):
            center = ref[b, here]
            return 0.25 * (ref[b, low] + ref[b, high] + left(center) + right(center))

        mean_u, mean_v = mean(u_prev), mean(v_prev)
        gx, gy = gx_r[b, here], gy_r[b, here]
        common = (gx * mean_u + gy * mean_v + gt_r[b, here]) * inv_r[b, here]
        return mean_u - gx * common, mean_v - gy * common

    def step(b, e, first, second, outside=False):
        k0, k1, k2, k3 = (lax.rem(e + RING - back, RING) for back in range(4))
        total[b, k0] = first + second
        shift[b, k0] = second - first
        center = total[b, k1]
        gx = 0.25 * (right(center) - left(center))
        gy = quarter * (total[b, k0] - total[b, k2])
        gt = shift[b, k1]
        inv = 1.0 / (1.0 + gx * gx + gy * gy)
        common = gt * inv
        gx_r[b, k1], gy_r[b, k1], gt_r[b, k1], inv_r[b, k1] = gx, gy, gt, inv
        u1_r[b, k1] = -gx * common
        v1_r[b, k1] = -gy * common
        u2, v2 = iterate(b, u1_r, v1_r, k3, k2, k1)
        if outside:
            u2, v2 = jnp.zeros_like(u2), jnp.zeros_like(v2)
        u2_r[b, k2], v2_r[b, k2] = u2, v2
        u3, v3 = iterate(b, u2_r, v2_r, k0, k3, k2)
        q = jnp.maximum(e - 6, 0)
        start = lax.rem(q, n) * frames + b * STRIP
        place = pl.ds(pl.multiple_of(start, STRIP), STRIP)
        gath[q // n, place, :] = u3.astype(jnp.bfloat16)
        filt[q // n, place, :] = v3.astype(jnp.bfloat16)

    def pair(b, ref, after_ref, row):
        first = ref[row, pl.ds(pl.multiple_of(b * STRIP, STRIP), STRIP), :].astype(jnp.float32)
        later = jnp.minimum(b + 1, strips - 1)
        later = pl.ds(pl.multiple_of(later * STRIP, STRIP), STRIP)
        inside = ref[row, later, :].astype(jnp.float32)[0:1]
        upcoming = jnp.where(b == strips - 1, after_ref[row], inside)
        second = jnp.where(at_last, upcoming, pltpu.roll(first, STRIP - 1, 0))
        return first, second

    def emit(q):
        def send(src, dst, sem):
            block = src.at[q // n, span(lax.rem(q, n))]
            pltpu.make_async_copy(block, dst.at[physical(q)], sem).start()

        send(gath, u_ref, so.at[0])
        send(filt, v_ref, so.at[1])

    def arrive(c):
        pltpu.make_async_copy(filt.at[c], filt.at[c], r2.at[c]).wait()
        landed = after.at[pl.ds(c * n, n)]
        pltpu.make_async_copy(landed, landed, r3.at[c]).wait()
        sent = filt.at[c, pl.ds(0, (n - 1) * frames)]
        pltpu.make_async_copy(sent, sent, s2.at[c]).wait()

    def to_side(src, dst, k):
        return pltpu.make_async_remote_copy(
            src_ref=src,
            dst_ref=dst,
            send_sem=sh.at[k],
            recv_sem=rh.at[k],
            device_id={"space": 1 - side},
            device_id_type=MESH,
        )

    def group(g):
        arrive(g)

        @pl.when(g == 0)
        def _():
            halo = (
                to_side(land.at[pl.ds(0, 3)], land_h, 0),
                to_side(after.at[pl.ds(0, 3)], after_h, 1),
            )
            for copy in halo:
                copy.start()
            for copy in halo:
                copy.wait()

        def strip(b, carry):
            @pl.when(g == 0)
            def _():
                def before(e, carry):
                    step(b, e, *pair(b, land_h, after_h, 2 - e))
                    return carry

                lax.fori_loop(0, 3, before, 0)

            def inner(i, carry):
                row = g * n + i
                step(b, row + 3, *pair(b, land, after, row))
                return carry

            lax.fori_loop(0, n, inner, 0)
            return carry

        lax.fori_loop(0, strips, strip, 0)

        def out(i, carry):
            q = g * n - 3 + i

            @pl.when(q >= 0)
            def _():
                emit(q)

            return carry

        lax.fori_loop(0, n, out, 0)

    def begin(m, carry):
        scatter(m)
        return carry

    lax.fori_loop(0, 2, begin, 0)

    def turn_of(c, carry):
        @pl.when(c < chunks)
        def _():
            work(c)

        m = (c + 1) // per_block + 1

        @pl.when(jnp.logical_and(lax.rem(c + 1, per_block) == 0, m < blocks))
        def _():
            scatter(m)

        @pl.when(c >= DELAY)
        def _():
            group(c - DELAY)

        return carry

    lax.fori_loop(0, chunks + DELAY, turn_of, 0)

    def finish(b, carry):
        zero = jnp.zeros((STRIP, columns), jnp.float32)
        for i in range(3):
            step(b, rows + 3 + i, zero, zero, outside=i == 2)
        return carry

    lax.fori_loop(0, strips, finish, 0)
    for i in range(3):
        emit(rows - 3 + i)

    def drain(c, carry):
        sent = filt.at[c, pl.ds(0, (n - 1) * frames)]
        pltpu.make_async_copy(sent, sent, s1.at[c]).wait()
        sent = after.at[pl.ds(0, n - 1)]
        pltpu.make_async_copy(sent, sent, s3.at[c]).wait()
        return carry

    lax.fori_loop(0, chunks, drain, 0)
    pltpu.make_async_copy(u_ref, u_ref, so.at[0]).wait()
    pltpu.make_async_copy(v_ref, v_ref, so.at[1]).wait()


def exchange_and_flow(frames, signal_power):
    n = lax.axis_size("tm")
    count, rows, columns = frames.shape
    chunks, half, strips = rows // n, F // 2, count // STRIP
    basis, inverse = real_basis()
    power = jnp.concatenate([signal_power, signal_power[1:half]], axis=0)
    power = jnp.broadcast_to(power[:, None], (F, TILE))
    vmem = pl.BlockSpec(memory_space=pltpu.VMEM)
    hbm = pl.BlockSpec(memory_space=pl.ANY)
    out = jax.ShapeDtypeStruct((rows, count, columns), jnp.bfloat16)
    dma = pltpu.SemaphoreType.DMA
    return pl.pallas_call(
        functools.partial(fused_kernel, n),
        out_shape=(out, out),
        in_specs=[hbm, vmem, vmem, vmem],
        out_specs=(hbm, hbm),
        scratch_shapes=[
            pltpu.VMEM((2, count, STRIP, columns), jnp.bfloat16),
            pltpu.VMEM((rows, count, columns), jnp.bfloat16),
            pltpu.VMEM((chunks, F, columns), jnp.bfloat16),
            pltpu.VMEM((chunks, F, columns), jnp.bfloat16),
            pltpu.VMEM((rows, count, columns), jnp.bfloat16),
            pltpu.VMEM((chunks, n, 1, columns), jnp.float32),
            pltpu.VMEM((rows, 1, columns), jnp.float32),
            pltpu.VMEM((3, count, columns), jnp.bfloat16),
            pltpu.VMEM((3, 1, columns), jnp.float32),
        ]
        + [pltpu.VMEM((strips, RING, STRIP, columns), jnp.float32)] * 10
        + [dma((2,))]
        + [dma((chunks,))] * 6
        + [dma((2,))] * 3,
        compiler_params=pltpu.CompilerParams(
            collective_id=0, has_side_effects=True, vmem_limit_bytes=60 * 2**20
        ),
        cost_estimate=pl.CostEstimate(
            flops=4 * F * rows * count * columns,
            bytes_accessed=6 * rows * count * columns,
            transcendentals=0,
        ),
        name="exchange",
    )(frames, jnp.asarray(basis), jnp.asarray(inverse), power)


def widen_kernel(u_in, v_in, u_out, v_out):
    for b in range(0, u_in.shape[2], TILE):
        cols = slice(b, b + TILE)
        u_out[:, :, cols] = jnp.swapaxes(u_in[:, :, cols].astype(jnp.float32), 0, 1)
        v_out[:, :, cols] = jnp.swapaxes(v_in[:, :, cols].astype(jnp.float32), 0, 1)


def widen(u, v):
    rows, count, columns = u.shape
    out = jax.ShapeDtypeStruct((count, rows, columns), jnp.float32)
    in_spec = pl.BlockSpec((STRIP, STRIP, columns), lambda i, j: (j, i, 0))
    out_spec = pl.BlockSpec((STRIP, STRIP, columns), lambda i, j: (i, j, 0))
    return pl.pallas_call(
        widen_kernel,
        grid=(count // STRIP, rows // STRIP),
        out_shape=(out, out),
        in_specs=[in_spec, in_spec],
        out_specs=(out_spec, out_spec),
        compiler_params=pltpu.CompilerParams(vmem_limit_bytes=60 * 2**20),
        cost_estimate=pl.CostEstimate(
            flops=0, bytes_accessed=12 * rows * count * columns, transcendentals=0
        ),
        name="widen",
    )(u, v)


def shards(frames, signal_power):
    n = lax.axis_size("tm")
    count, rows, columns = frames.shape
    fits = n >= 3 and count % STRIP == 0 and rows % (2 * STRIP) == 0 and rows % n == 0
    fits = fits and STRIP % n == 0 and columns % TILE == 0 and lax.axis_size("space") == 2
    if not fits:
        return plain_shards(frames, signal_power)
    return widen(*exchange_and_flow(frames, signal_power))


def solution(mesh):
    in_specs = (P("tm", ("band", "space"), None), P())
    out_specs = (P("tm", ("band", "space"), None), P("tm", ("band", "space"), None))
    return jax.shard_map(shards, mesh=mesh, in_specs=in_specs, out_specs=out_specs, check_vma=False)
```
